256 devices in a mesh: worker: 8 (over z_lo, x), shard: 32 (over z_hi, y, core).
Axes of the slice: x: 4, y: 4, z: 8 (z_hi: 4, z_lo: 2; z = z_hi * 2 + z_lo), core: 2. Of those that a mesh axis runs over, the one named last changes fastest.
Arguments:
- acts: bfloat16 [131072, 8192], P(('worker', 'shard')), may hold values from -6 to 6
- out_grads: bfloat16 [131072, 1024], P(('worker', 'shard')), may hold values from -24 to 24
- local_weight: bfloat16 [8, 1024, 8192], P('worker', 'shard'), may hold values from -6.1 to 6.1
- adam_mean: float32 [8, 1024, 8192], P('worker', 'shard'), may hold values from -0.6 to 0.6
- adam_var: float32 [8, 1024, 8192], P('worker', 'shard'), may hold values from 0.05 to 2
- global_weight: float32 [1024, 8192], P('shard', 'worker'), may hold values from -6 to 6
- outer_momentum: float32 [1024, 8192], P('shard', 'worker'), may hold values from -0.12 to 0.12
- step_count: int32 [1], replicated, may hold values from 1 to 8
Outputs:
- synced_weight: bfloat16 [1024, 8192], P('shard')
- new_global: float32 [1024, 8192], P('shard', 'worker')
- new_momentum: float32 [1024, 8192], P('shard', 'worker')
The draws below stay inside these ranges and needn't reach their ends.
All inputs are finite; a program needn't handle non-finite values.
Results may differ from the reference program's by a relative error of at most 0.012.
Values may be sent and summed in bfloat16 or wider, within the bound.
No kernel may reach another device: no remote copies, remote signals or barrier semaphores. Data moves between devices by JAX's collectives and lax.ppermute only.
A program may use at most 128 MiB of HBM per device.

```python
import math
import jax
import jax.numpy as jnp
from jax import lax

D = 8192
KV = 1024
TOK_DEV = 512
TOKENS = 131072
N_WORKER = 8
N_SHARD = 32


def shared_anchor(key):
    return jnp.clip(jax.random.normal(key, (KV, D), jnp.float32), -6.0, 6.0)


def draw_global_weight(key, part):
    anchor = shared_anchor(key)
    return anchor.astype(jnp.float32)


def draw_local_weight(key, part):
    anchor = shared_anchor(key)
    key = jax.random.fold_in(key, 5)
    drift = jnp.clip(0.015 * jax.random.normal(key, (N_WORKER, KV, D), jnp.float32), -0.09, 0.09)
    return (anchor[None] + drift).astype(jnp.bfloat16)


def with_spikes(array, own_key, source, target, blocks, factor):
    def block_of(dim):
        return (jnp.arange(array.shape[dim]) // (array.shape[dim] // blocks)).reshape((-1,) + (1,) * (array.ndim - 1 - dim))

    near = jax.random.permutation(own_key, blocks)[block_of(target)]
    other_side = (block_of(target) + blocks // 2) % blocks
    return jnp.where((block_of(source) == near) | (block_of(source) == other_side), factor * array, array)


def block_scale(key, shape, pieces, least, largest):
    level = 1.0
    for position, blocks in pieces:
        draws = jax.random.uniform(jax.random.fold_in(jax.random.fold_in(key, 6), position), (blocks,), jnp.float32, least / len(pieces), largest / len(pieces))
        level = level * jnp.repeat(jnp.exp(draws), shape[position] // blocks).reshape((-1,) + (1,) * (len(shape) - 1 - position))
    return level


def bell_draw(rng, shape, deviation, limit, pieces=(), dtype=jnp.bfloat16):
    result = deviation * jax.random.normal(rng, shape, jnp.float32)
    if pieces:
        result = result * block_scale(rng, shape, pieces, -0.22, 0.18)
    return jnp.clip(result, -limit, limit).astype(dtype)


def gaussian_with(rng, extent, deviation, bound, shards, heavy, dtype=jnp.bfloat16):
    result = deviation * jax.random.normal(rng, extent, jnp.float32)
    if shards:
        result = result * block_scale(rng, extent, shards, -0.22, 0.18)
    return jnp.clip(with_spikes(result, jax.random.fold_in(rng, 3), *heavy), -bound, bound).astype(dtype)


def setup_inputs(seed: int = 0) -> dict:
    arg_keys = jax.random.split(jax.random.key(seed), 9)
    acts = bell_draw(arg_keys[0], (TOKENS, D), 1.0, 6.0, ((0, 256),))
    out_grads = gaussian_with(arg_keys[1], (TOKENS, KV), 1.0, 24.0, ((0, 256),), (0, 1, 256, 6.0))
    local_weight = draw_local_weight(jax.random.fold_in(arg_keys[8], 71), 0)
    adam_mean = bell_draw(arg_keys[3], (N_WORKER, KV, D), 0.1, 0.6, ((0, 8), (1, 32)), jnp.float32)
    adam_var = jnp.clip(jnp.exp(math.log(2.0) - 3.6888794 * jax.random.uniform(arg_keys[4], (N_WORKER, KV, D), jnp.float32) ** block_scale(arg_keys[4], (N_WORKER, KV, D), ((0, 8), (1, 32)), -0.2, 0.2)), 0.05, 2.0)
    global_weight = draw_global_weight(jax.random.fold_in(arg_keys[8], 71), 0)
    outer_momentum = bell_draw(arg_keys[6], (KV, D), 0.02, 0.12, ((0, 32), (1, 8)), jnp.float32)
    step_count = jax.random.randint(arg_keys[7], (1,), 1, 9).astype(jnp.int32)
    return {"acts": acts, "out_grads": out_grads, "local_weight": local_weight, "adam_mean": adam_mean, "adam_var": adam_var, "global_weight": global_weight, "outer_momentum": outer_momentum, "step_count": step_count}


def inner_step(weight, mean, var, grad, count):
    moment = 0.9 * mean + 0.1 * grad
    second = 0.95 * var + 0.05 * grad * grad
    first_fix = 1.0 - jnp.power(0.9, count)
    second_fix = 1.0 - jnp.power(0.95, count)
    ratio = moment / first_fix / (jnp.sqrt(second / second_fix) + 1e-08)
    return weight - 0.1 * (ratio + 0.1 * weight)

def reference(acts, out_grads, local_weight, adam_mean, adam_var, global_weight, outer_momentum, step_count):
    wtok = TOK_DEV * N_SHARD
    factor = 1.0 / math.sqrt(wtok)
    count = step_count[0].astype(jnp.float32)
    total = jnp.zeros((KV, D), jnp.float32)
    for replica in range(N_WORKER):
        inputs = acts[replica * wtok:(replica + 1) * wtok].reshape(N_SHARD, TOK_DEV, D)
        upstream = out_grads[replica * wtok:(replica + 1) * wtok].reshape(N_SHARD, TOK_DEV, KV)

        def add_block(carry, pair):
            block_in, block_up = pair
            term = lax.dot_general(block_up, block_in, (((0,), (0,)), ((), ())), preferred_element_type=jnp.float32) * factor
            term = lax.optimization_barrier(term.astype(jnp.bfloat16))
            return (carry + term.astype(jnp.float32), None)
        grad, _ = lax.scan(add_block, jnp.zeros((KV, D), jnp.float32), (inputs, upstream))
        weight = local_weight[replica].astype(jnp.float32)
        total = total + inner_step(weight, adam_mean[replica], adam_var[replica], grad, count)
    delta = global_weight - total / N_WORKER
    new_momentum = 0.9 * outer_momentum + delta
    new_global = global_weight - 0.7 * (delta + 0.9 * new_momentum)
    return (new_global.astype(jnp.bfloat16), new_global, new_momentum)
```

```python
import functools
import math

import jax
import jax.numpy as jnp
from jax import lax
from jax.experimental import pallas as pl
from jax.experimental.pallas import tpu as pltpu
from jax.sharding import PartitionSpec as P

WIDTHS = {"a": 2304, "b": 2304, "c": 1024, "d": 1024, "e": 1536}

NZ, NY, NC = 4, 4, 2
SHARDS = NZ * NY * NC
BACK = (1, 2, 3, 0)
VMEM = pl.BlockSpec(memory_space=pltpu.VMEM)
LIMIT = 16 << 20
bf16, f32 = jnp.bfloat16, jnp.float32


def shard_of(z, y, c):
    return (z % NZ * NY + y % NY) * NC + c % NC


def sense(c):
    return 1 if c == 0 else -1


def move(array, axis, steps=1):
    pairs = []
    for z in range(NZ):
        for y in range(NY):
            for c in range(NC):
                by = steps * sense(c)
                to = {
                    "z": shard_of(z + by, y, c), "y": shard_of(z, y + by, c), "core": shard_of(z, y, c + 1)
                }[axis]
                pairs.append((shard_of(z, y, c), to))
    return lax.ppermute(array, "shard", pairs)


class Line:
    def __init__(self):
        self.last = None

    def call(self, kernel, name, outs, *operands, scalars=(), flops=0):
        size = sum(o.size * o.dtype.itemsize for o in operands) + sum(
            math.prod(s) * jnp.dtype(t).itemsize for s, t in outs
        )
        before = () if self.last is None else (self.last,)
        skip = len(before)
        results = pl.pallas_call(
            lambda *refs: kernel(*refs[skip:]),
            out_shape=[jax.ShapeDtypeStruct(s, t) for s, t in outs],
            in_specs=[pl.BlockSpec(memory_space=pl.ANY)] * skip
            + [pl.BlockSpec(memory_space=pltpu.SMEM)] * len(scalars)
            + [VMEM] * len(operands),
            out_specs=[VMEM] * len(outs),
            compiler_params=pltpu.CompilerParams(vmem_limit_bytes=LIMIT),
            cost_estimate=pl.CostEstimate(flops=0, bytes_accessed=0, transcendentals=0),
            name=name,
        )(*before, *scalars, *operands)
        self.last = results[0]
        return results


def pick_kernel(factor, feature_ref, grads_ref, out_ref):
    shape = (feature_ref.shape[0], grads_ref.shape[1])
    match = feature_ref[...] == lax.broadcasted_iota(jnp.int32, shape, 1)
    pick = jnp.where(match, factor, 0.0).astype(bf16)
    out_ref[...] = lax.dot_general(
        pick, grads_ref[...], (((1,), (1,)), ((), ())), preferred_element_type=f32
    ).astype(bf16)


def product_kernel(split, gm_ref, gs_ref, mine_ref, sib_ref, *outs):
    cols = mine_ref.shape[1]
    tile = 256
    for start in range(0, cols, tile):
        part = pl.ds(start, tile)
        mine, sib = mine_ref[:, part], sib_ref[:, part]
        total = jnp.dot(gm_ref[...], mine, preferred_element_type=f32)
        total += jnp.dot(gs_ref[...], sib, preferred_element_type=f32)
        for out, rows in zip(outs, split):
            out[:, part] = jnp.concatenate([total[r] for r in rows], axis=0).astype(out.dtype)


def relay_kernel(keep_ref, came_ref, out_ref):
    out_ref[...] = (keep_ref[...] + came_ref[...].astype(f32)).astype(bf16)


def settle_kernel(n, *refs):
    ins, outs = refs[:2 * n], refs[2 * n:]
    start = 0
    for own, came in zip(ins[::2], ins[1::2]):
        part = slice(start, start + own.shape[1])
        start += own.shape[1]
        rows = own.shape[0] // len(outs)
        for i, out in enumerate(outs):
            at = slice(i * rows, (i + 1) * rows)
            out[:, part] = (own[at] + came[at].astype(f32)).astype(out.dtype)


def adam_kernel(start, fix_ref, weight_ref, mean_ref, var_ref, own_ref, *refs):
    came, out_ref = refs[:-1], refs[-1]
    at = pl.ds(start, own_ref.shape[1])
    grad = own_ref[...]
    for ref in came:
        grad += ref[...].astype(f32)
    weight = weight_ref[:, at].astype(f32)
    moment = 0.9 * mean_ref[:, at] + 0.1 * grad
    second = 0.95 * var_ref[:, at] + 0.05 * grad * grad
    ratio = moment / fix_ref[0] / (jnp.sqrt(second / fix_ref[1]) + 1e-08)
    out_ref[...] = weight - 0.1 * (ratio + 0.1 * weight)


def after(array, *others):
    return lax.optimization_barrier((array,) + others)[0]


def local(acts, out_grads, local_weight, adam_mean, adam_var, global_weight, outer_momentum, step_count):
    workers = lax.axis_size("worker")
    tokens, width = acts.shape
    features = out_grads.shape[1]
    share = features // SHARDS
    half = features // NC
    rows = half // NY
    factor = 1.0 / math.sqrt(tokens * SHARDS)
    count = step_count[0].astype(f32)
    index = lax.axis_index("shard")
    core, y, z = index % NC, (index // NC) % NY, index // (NC * NY)

    offsets, total = {}, 0
    for k, cols in WIDTHS.items():
        offsets[k] = total
        total += cols

    back = jnp.array(BACK, jnp.int32) * jnp.where(core == 0, 1, -1)
    owner = ((z - back[None, :]) % NZ * NY + (y - back[:, None]) % NY) * NC + core
    feature = (owner.reshape(-1, 1) * share + jnp.arange(share, dtype=jnp.int32)[None, :]).reshape(half, 1)
    fix = jnp.stack([1.0 - jnp.power(0.9, count), 1.0 - jnp.power(0.95, count)])
    line = Line()

    def picked(grads):
        return line.call(
            functools.partial(pick_kernel, factor), "pick", [((half, tokens), bf16)], feature, grads
        )[0]

    mine, sib, blocks, flying = ({} for _ in range(4))
    weights = (local_weight[0], adam_mean[0], adam_var[0])
    by_y = [[slice(i * rows, (i + 1) * rows)] for i in range(NY)]
    by_z = [[slice((j * NZ + i) * share, (j * NZ + i + 1) * share) for j in range(NY)] for i in range(NZ)]

    def fetch(k, *others):
        mine[k] = lax.slice_in_dim(after(acts, *others), offsets[k], offsets[k] + WIDTHS[k], axis=1)
        sib[k] = move(mine[k], "core")

    def send(k, message, axis):
        flying[k] = move(message, axis)

    def produce(k, axis):
        out = ((rows, WIDTHS[k]), bf16), *[((rows, WIDTHS[k]), f32)] * 3
        message, *blocks[k] = line.call(
            functools.partial(product_kernel, by_y if axis == "y" else by_z), "product", out,
            gm, gs, mine[k], sib[k],
        )
        send(k, message, axis)

    def relay(k, axis):
        keep = blocks[k].pop(0)
        send(k, line.call(relay_kernel, "relay", [(keep.shape, bf16)], keep, flying[k])[0], axis)

    def settle(ks, axis, direct=False):
        cols = sum(WIDTHS[k] for k in ks)
        out = [((share, cols), bf16)] + [((share, cols), bf16 if direct else f32)] * 2 + [((share, cols), f32)]
        message, *blocks[ks] = line.call(
            functools.partial(settle_kernel, len(ks)), "settle", out,
            *[a for k in ks for a in (blocks[k][0], flying[k])],
        )
        if direct:
            far = [move(m, axis, -b) for m, b in zip((message, *blocks[ks][:2]), BACK)]
            blocks[ks] = blocks[ks][2:]
            flying[ks] = far
        else:
            send(ks, message, axis)

    stepped = {}

    def adam(ks):
        own, = blocks[ks]
        came = flying[ks] if isinstance(flying[ks], list) else [flying[ks]]
        stepped[offsets[ks[0]]] = line.call(
            functools.partial(adam_kernel, offsets[ks[0]]), "adam", [(own.shape, f32)],
            *weights, own, *came, scalars=(fix,),
        )[0]

    fetch("a")
    sib_grads = move(out_grads, "core")
    gm = picked(out_grads)
    fetch("b", gm)
    gs = picked(sib_grads)
    fetch("e", gs)
    produce("a", "y")
    fetch("c", blocks["a"][0])
    produce("b", "y")
    fetch("d", blocks["b"][0])
    produce("e", "z")
    relay("a", "y")
    relay("b", "y")
    relay("e", "z")
    relay("a", "y")
    relay("b", "y")
    relay("e", "z")
    produce("c", "y")
    produce("d", "y")
    settle("ab", "z")
    relay("c", "y")
    relay("d", "y")
    settle("e", "y")
    relay("ab", "z")
    relay("c", "y")
    relay("d", "y")
    relay("e", "y")
    relay("ab", "z")
    settle("cd", "z", direct=True)
    relay("e", "y")
    adam("ab")
    adam("e")
    adam("cd")
    stepped = [stepped[k] for k in sorted(stepped)]
    stepped = jnp.concatenate(stepped, axis=1)
    wide = width // workers
    parts = lax.all_to_all(stepped, "worker", split_axis=1, concat_axis=0, tiled=True)
    delta = global_weight - jnp.sum(parts.reshape(workers, share, wide), axis=0) / workers
    momentum = 0.9 * outer_momentum + delta
    updated = global_weight - 0.7 * (delta + 0.9 * momentum)
    piece = updated.astype(bf16)
    spread = jnp.broadcast_to(piece[None], (workers,) + piece.shape).reshape(workers * share, wide)
    synced = lax.all_to_all(spread, "worker", split_axis=0, concat_axis=1, tiled=True)
    return (synced, updated, momentum)


def solution(mesh):
    placed = (
        P(("worker", "shard"), None),
        P(("worker", "shard"), None),
        P("worker", "shard", None),
        P("worker", "shard", None),
        P("worker", "shard", None),
        P("shard", "worker"),
        P("shard", "worker"),
        P(),
    )
    return jax.shard_map(
        local,
        mesh=mesh,
        in_specs=placed,
        out_specs=(P("shard", None), P("shard", "worker"), P("shard", "worker")),
        check_vma=False,
    )
```

```python
import functools
import math

import jax
import jax.numpy as jnp
from jax import lax
from jax.experimental import pallas as pl
from jax.experimental.pallas import tpu as pltpu
from jax.sharding import PartitionSpec as P

WIDTHS = {"a": 2048, "b": 2048, "e": 1536, "c": 1536, "d": 1024}
TILE = 512


NZ, NY, NC = 4, 4, 2
SHARDS = NZ * NY * NC
BACK = (1, 2, 3, 0)
VMEM = pl.BlockSpec(memory_space=pltpu.VMEM)
ANY = pl.BlockSpec(memory_space=pl.ANY)
LIMIT = 12 << 20
COST = {"product": 50_000_000_000, "pick": 50_000_000_000}
OTHER_COST = 2_000_000_000
LATE_COST = 500_000_000
bf16, f32 = jnp.bfloat16, jnp.float32


def shard_of(z, y, c):
    return (z % NZ * NY + y % NY) * NC + c % NC


def sense(c):
    return 1 if c == 0 else -1


def move(array, axis, steps=1):
    pairs = []
    for z in range(NZ):
        for y in range(NY):
            for c in range(NC):
                by = steps * sense(c)
                to = {
                    "z": shard_of(z + by, y, c), "y": shard_of(z, y + by, c), "core": shard_of(z, y, c + 1)
                }[axis]
                pairs.append((shard_of(z, y, c), to))
    return lax.ppermute(array, "shard", pairs)


class Line:
    def __init__(self):
        self.last = None

    def call(self, name, *parts, scalars=(), **more):
        before = () if self.last is None else (self.last,)
        lead = len(before) + len(scalars)
        outs = [o for _, out, _ in parts for o in out]
        operands = [o for _, _, ins in parts for o in ins]

        def body(*refs):
            given, made, scratch = lead, lead + len(operands), refs[lead + len(operands) + len(outs):]
            for kernel, out, ins in parts:
                kernel(
                    *refs[len(before):lead], *refs[given:given + len(ins)], *refs[made:made + len(out)], *scratch
                )
                given, made = given + len(ins), made + len(out)

        flops = more.get("cost", COST.get(name, OTHER_COST))
        results = pl.pallas_call(
            body,
            out_shape=[jax.ShapeDtypeStruct(s, t) for s, t in outs],
            in_specs=[ANY] * len(before)
            + [pl.BlockSpec(memory_space=pltpu.SMEM)] * len(scalars)
            + (more.get("specs") or [VMEM] * len(operands)),
            out_specs=more.get("out_specs") or [VMEM] * len(outs),
            scratch_shapes=more.get("scratch", ()),
            grid=more.get("grid", ()),
            compiler_params=pltpu.CompilerParams(vmem_limit_bytes=more.get("limit", LIMIT)),
            cost_estimate=pl.CostEstimate(flops=flops, bytes_accessed=flops // 100, transcendentals=0),
            name=name,
        )(*before, *scalars, *operands)
        self.last = results[0]
        split, at = [], 0
        for _, out, _ in parts:
            split.append(results[at:at + len(out)])
            at += len(out)
        return split


def pick_kernel(share, factor, grads_ref, *outs):
    index = lax.axis_index("shard")
    y, z = (index // NC) % NY, index // (NC * NY)
    for out_ref, core in zip(outs, (index % NC, 1 - index % NC)):
        way = 1 - 2 * core
        row = lax.broadcasted_iota(jnp.int32, (out_ref.shape[0], 1), 0)
        block = row // share
        back_y, back_z = (block // NZ + 1) % NY, (block % NZ + 1) % NZ
        owner = ((z + NZ - way * back_z) % NZ * NY + (y + NY - way * back_y) % NY) * NC + core
        feature = owner * share + row % share
        place = lax.broadcasted_iota(jnp.int32, (out_ref.shape[0], grads_ref.shape[1]), 1)
        pick = jnp.where(feature == place, factor, 0.0).astype(bf16)
        out_ref[...] = lax.dot_general(
            pick, grads_ref[...], (((1,), (1,)), ((), ())), preferred_element_type=f32
        ).astype(bf16)


def product_kernel(split, first, mine_rows, sib_rows, acts_ref, mine_ref, sib_ref, held, sems):
    copies = [
        pltpu.make_async_copy(acts_ref.at[:, pl.ds(first + i * TILE, TILE)], held.at[i], sems.at[i])
        for i in range(held.shape[0])
    ]
    for copy in copies:
        copy.start()
    for i, copy in enumerate(copies):
        copy.wait()
        for start in range(0, TILE, TILE // 2):
            tile = held[i, :, start:start + TILE // 2]
            for rows_ref, out in ((sib_rows, sib_ref), (mine_rows, mine_ref)):
                total = jnp.dot(rows_ref[...], tile, preferred_element_type=f32).astype(bf16)
                at = pl.ds(i * TILE + start, TILE // 2)
                out[:, at] = jnp.concatenate([total[r] for rows in split for r in rows], axis=0)


def sum_of(at, terms):
    total = 0.0
    for ref, whole in terms:
        total += (ref[...] if whole else ref[at]).astype(f32)
    return total


def relay_kernel(at, wholes, *refs):
    refs[-1][...] = sum_of(at, zip(refs, wholes)).astype(bf16)


def settle_kernel(at, wholes, n, *refs):
    each = len(wholes)
    outs = refs[each * n:]
    start = 0
    for i in range(n):
        ins = refs[each * i:each * (i + 1)]
        part = slice(start, start + ins[0].shape[1])
        start += ins[0].shape[1]
        total = sum_of(at, zip(ins, wholes))
        row = 0
        for out in outs:
            out[:, part] = total[row:row + out.shape[0]].astype(out.dtype)
            row += out.shape[0]


def adam_kernel(start, fix_ref, weight_ref, mean_ref, var_ref, own_ref, *refs):
    came, out_ref = refs[:-1], refs[-1]
    at = pl.ds(start, own_ref.shape[1])
    grad = own_ref[own_ref.shape[0] - out_ref.shape[0]:].astype(f32)
    for ref in came:
        grad += ref[...].astype(f32)
    weight = weight_ref[:, at].astype(f32)
    moment = 0.9 * mean_ref[:, at] + 0.1 * grad
    second = 0.95 * var_ref[:, at] + 0.05 * grad * grad
    ratio = moment / fix_ref[0] / (jnp.sqrt(second / fix_ref[1]) + 1e-08)
    out_ref[...] = weight - 0.1 * (ratio + 0.1 * weight)


def local(acts, out_grads, local_weight, adam_mean, adam_var, global_weight, outer_momentum, step_count):
    workers = lax.axis_size("worker")
    tokens, width = acts.shape
    features = out_grads.shape[1]
    share = features // SHARDS
    half = features // NC
    rows = half // NY
    factor = 1.0 / math.sqrt(tokens * SHARDS)
    count = step_count[0].astype(f32)
    offsets, total = {}, 0
    for k, cols in WIDTHS.items():
        offsets[k] = total
        total += cols

    fix = jnp.stack([1.0 - jnp.power(0.9, count), 1.0 - jnp.power(0.95, count)])
    line = Line()

    blocks, sent, flying = {}, {}, {}
    weights = (local_weight[0], adam_mean[0], adam_var[0])
    by_y = [[slice(i * rows, (i + 1) * rows)] for i in range(NY)]
    by_z = [[slice((j * NZ + i) * share, (j * NZ + i + 1) * share) for j in range(NY)] for i in range(NZ)]

    def produce(k):
        kernel = functools.partial(product_kernel, by_z if k == "e" else by_y, offsets[k])
        tiles = WIDTHS[k] // TILE
        (made, other), = line.call(
            "product", (kernel, [((half, WIDTHS[k]), bf16)] * 2, (mine_rows, sib_rows, acts)), specs=[VMEM, VMEM, ANY],
            scratch=[pltpu.VMEM((tiles, tokens, TILE), bf16), pltpu.SemaphoreType.DMA((tiles,))],
        )
        blocks[k], sent[k], flying[k] = [made, move(other, "core")], 0, None

    def terms(k):
        size = {half: rows, 3 * share: share}[blocks[k][0].shape[0]]
        at = slice(sent[k] * size, (sent[k] + 1) * size)
        came = [] if flying[k] is None else [flying[k]]
        return at, [False] * len(blocks[k]) + [True] * len(came), [*blocks[k], *came]

    def relay(k, axis):
        at, wholes, ins = terms(k)
        shape = at.stop - at.start, ins[0].shape[1]

        def done(made):
            flying[k] = move(made[0], axis)
            sent[k] += 1

        return functools.partial(relay_kernel, at, wholes), [(shape, bf16)], ins, done

    def settle(ks, axis, direct=False):
        cols = sum(WIDTHS[k] for k in ks)
        at, wholes, _ = terms(ks[0])
        ins = [a for k in ks for a in terms(k)[2]]
        if direct:
            out = [((share, cols), bf16)] * 3 + [((share, cols), f32)]
        else:
            out = [((share, cols), bf16), ((3 * share, cols), bf16)]

        def done(made):
            if direct:
                flying[ks] = [move(m, axis, -b) for m, b in zip(made, BACK[:3])]
                blocks[ks], sent[ks] = [made[3]], None
            else:
                flying[ks], blocks[ks], sent[ks] = move(made[0], axis), [made[1]], 0

        return functools.partial(settle_kernel, at, wholes, len(ks)), out, ins, done

    stepped = {}

    def adam(ks):
        start, cols = offsets[ks[0]], sum(WIDTHS[k] for k in ks)
        came = flying[ks] if sent[ks] is None else [flying[ks]]
        last = functools.partial(adam_kernel, start)

        def done(made):
            stepped[start] = made[0]

        return last, [((share, cols), f32)], (*weights, blocks[ks][0], *came), done

    def run(name, *parts, **more):
        results = line.call(name, *[p[:3] for p in parts], **more)
        for made, part in zip(results, parts):
            part[3](made)
        return results[-1]

    (mine_rows, sib_rows), = line.call(
        "pick", (functools.partial(pick_kernel, share, factor), [((half, tokens), bf16)] * 2, (out_grads,))
    )
    produce("a")
    produce("b")
    run("relay", relay("a", "y"))
    produce("e")
    run("relay", relay("b", "y"))
    run("relay", relay("e", "z"))
    produce("c")
    produce("d")
    run("relay", relay("a", "y"))
    run("relay", relay("b", "y"))
    run("relay", relay("e", "z"))
    run("relay", relay("a", "y"))
    run("relay", relay("b", "y"))
    run("relay", relay("c", "y"))
    run("relay", relay("e", "z"))
    run("relay", relay("d", "y"))
    run("settle", settle("ab", "z"))
    run("relay", relay("c", "y"))
    run("relay", relay("d", "y"))
    run("settle", settle("e", "y"))
    run("relay", relay("ab", "z"))
    run("relay", relay("c", "y"), cost=LATE_COST)
    run("relay", relay("e", "y"), cost=LATE_COST)
    run("relay", relay("d", "y"), cost=LATE_COST)
    run("relay", relay("ab", "z"), cost=LATE_COST)
    run("settle", settle("cd", "z", direct=True), cost=LATE_COST)
    run("relay", relay("e", "y"), cost=LATE_COST)
    run("adam", adam("ab"), scalars=(fix,))
    run("adam", adam("e"), scalars=(fix,))
    run("adam", adam("cd"), scalars=(fix,))
    stepped = [stepped[k] for k in sorted(stepped)]
    stepped = jnp.concatenate(stepped, axis=1)
    wide = width // workers
    parts = lax.all_to_all(stepped, "worker", split_axis=1, concat_axis=0, tiled=True)
    delta = global_weight - jnp.sum(parts.reshape(workers, share, wide), axis=0) / workers
    momentum = 0.9 * outer_momentum + delta
    updated = global_weight - 0.7 * (delta + 0.9 * momentum)
    piece = updated.astype(bf16)
    spread = jnp.broadcast_to(piece[None], (workers,) + piece.shape).reshape(workers * share, wide)
    synced = lax.all_to_all(spread, "worker", split_axis=0, concat_axis=1, tiled=True)
    return (synced, updated, momentum)


def solution(mesh):
    placed = (
        P(("worker", "shard"), None),
        P(("worker", "shard"), None),
        P("worker", "shard", None),
        P("worker", "shard", None),
        P("worker", "shard", None),
        P("shard", "worker"),
        P("shard", "worker"),
        P(),
    )
    return jax.shard_map(
        local,
        mesh=mesh,
        in_specs=placed,
        out_specs=(P("shard", None), P("shard", "worker"), P("shard", "worker")),
        check_vma=False,
    )
```

```python
import functools
import math

import jax
import jax.numpy as jnp
from jax import lax
from jax.experimental import pallas as pl
from jax.experimental.pallas import tpu as pltpu
from jax.sharding import PartitionSpec as P

WIDTHS = {"a": 2048, "b": 2048, "e": 1536, "c": 1536, "d": 1024}
TILE = 512


NZ, NY, NC = 4, 4, 2
SHARDS = NZ * NY * NC
BACK = (1, 2, 3, 0)
VMEM = pl.BlockSpec(memory_space=pltpu.VMEM)
ANY = pl.BlockSpec(memory_space=pl.ANY)
LIMIT = 12 << 20
COST = {"product": 50_000_000_000, "pick": 50_000_000_000}
OTHER_COST = 2_000_000_000
LATE_COST = 500_000_000
bf16, f32 = jnp.bfloat16, jnp.float32


def shard_of(z, y, c):
    return (z % NZ * NY + y % NY) * NC + c % NC


def sense(c):
    return 1 if c == 0 else -1


def move(array, axis, steps=1):
    pairs = []
    for z in range(NZ):
        for y in range(NY):
            for c in range(NC):
                by = steps * sense(c)
                to = {
                    "z": shard_of(z + by, y, c), "y": shard_of(z, y + by, c), "core": shard_of(z, y, c + 1)
                }[axis]
                pairs.append((shard_of(z, y, c), to))
    return lax.ppermute(array, "shard", pairs)


class Line:
    def __init__(self):
        self.last = None

    def call(self, name, *parts, scalars=(), **more):
        before = () if self.last is None else (self.last,)
        lead = len(before) + len(scalars)
        outs = [o for _, out, _ in parts for o in out]
        operands = [o for _, _, ins in parts for o in ins]

        def body(*refs):
            given, made, scratch = lead, lead + len(operands), refs[lead + len(operands) + len(outs):]
            for kernel, out, ins in parts:
                kernel(
                    *refs[len(before):lead], *refs[given:given + len(ins)], *refs[made:made + len(out)], *scratch
                )
                given, made = given + len(ins), made + len(out)

        flops = more.get("cost", COST.get(name, OTHER_COST))
        results = pl.pallas_call(
            body,
            out_shape=[jax.ShapeDtypeStruct(s, t) for s, t in outs],
            in_specs=[ANY] * len(before)
            + [pl.BlockSpec(memory_space=pltpu.SMEM)] * len(scalars)
            + (more.get("specs") or [VMEM] * len(operands)),
            out_specs=more.get("out_specs") or [VMEM] * len(outs),
            scratch_shapes=more.get("scratch", ()),
            grid=more.get("grid", ()),
            compiler_params=pltpu.CompilerParams(vmem_limit_bytes=more.get("limit", LIMIT)),
            cost_estimate=pl.CostEstimate(flops=flops, bytes_accessed=flops // 100, transcendentals=0),
            name=name,
        )(*before, *scalars, *operands)
        self.last = results[0]
        split, at = [], 0
        for _, out, _ in parts:
            split.append(results[at:at + len(out)])
            at += len(out)
        return split


def pick_kernel(share, factor, grads_ref, *outs):
    index = lax.axis_index("shard")
    y, z = (index // NC) % NY, index // (NC * NY)
    for out_ref, core in zip(outs, (index % NC, 1 - index % NC)):
        way = 1 - 2 * core
        row = lax.broadcasted_iota(jnp.int32, (out_ref.shape[0], 1), 0)
        block = row // share
        back_y, back_z = (block // NZ + 1) % NY, (block % NZ + 1) % NZ
        owner = ((z + NZ - way * back_z) % NZ * NY + (y + NY - way * back_y) % NY) * NC + core
        feature = owner * share + row % share
        place = lax.broadcasted_iota(jnp.int32, (out_ref.shape[0], grads_ref.shape[1]), 1)
        pick = jnp.where(feature == place, factor, 0.0).astype(bf16)
        out_ref[...] = lax.dot_general(
            pick, grads_ref[...], (((1,), (1,)), ((), ())), preferred_element_type=f32
        ).astype(bf16)


def product_kernel(split, first, mine_rows, sib_rows, acts_ref, mine_ref, sib_ref, held, sems):
    copies = [
        pltpu.make_async_copy(acts_ref.at[:, pl.ds(first + i * TILE, TILE)], held.at[i], sems.at[i])
        for i in range(held.shape[0])
    ]
    for copy in copies:
        copy.start()
    for i, copy in enumerate(copies):
        copy.wait()
        for start in range(0, TILE, TILE // 2):
            tile = held[i, :, start:start + TILE // 2]
            for rows_ref, out in ((sib_rows, sib_ref), (mine_rows, mine_ref)):
                total = jnp.dot(rows_ref[...], tile, preferred_element_type=f32).astype(bf16)
                at = pl.ds(i * TILE + start, TILE // 2)
                out[:, at] = jnp.concatenate([total[r] for rows in split for r in rows], axis=0)


def sum_of(at, terms):
    total = 0.0
    for ref, whole in terms:
        total += (ref[...] if whole else ref[at]).astype(f32)
    return total


def relay_kernel(at, wholes, *refs):
    refs[-1][...] = sum_of(at, zip(refs, wholes)).astype(bf16)


def settle_kernel(at, wholes, n, *refs):
    each = len(wholes)
    outs = refs[each * n:]
    start = 0
    for i in range(n):
        ins = refs[each * i:each * (i + 1)]
        part = slice(start, start + ins[0].shape[1])
        start += ins[0].shape[1]
        total = sum_of(at, zip(ins, wholes))
        row = 0
        for out in outs:
            out[:, part] = total[row:row + out.shape[0]].astype(out.dtype)
            row += out.shape[0]


def adam_kernel(start, fix_ref, weight_ref, mean_ref, var_ref, own_ref, *refs):
    came, out_ref = refs[:-1], refs[-1]
    at = pl.ds(start, own_ref.shape[1])
    grad = own_ref[own_ref.shape[0] - out_ref.shape[0]:].astype(f32)
    for ref in came:
        grad += ref[...].astype(f32)
    weight = weight_ref[:, at].astype(f32)
    moment = 0.9 * mean_ref[:, at] + 0.1 * grad
    second = 0.95 * var_ref[:, at] + 0.05 * grad * grad
    ratio = moment / fix_ref[0] / (jnp.sqrt(second / fix_ref[1]) + 1e-08)
    out_ref[...] = weight - 0.1 * (ratio + 0.1 * weight)


def local(acts, out_grads, local_weight, adam_mean, adam_var, global_weight, outer_momentum, step_count):
    workers = lax.axis_size("worker")
    tokens, width = acts.shape
    features = out_grads.shape[1]
    share = features // SHARDS
    half = features // NC
    rows = half // NY
    factor = 1.0 / math.sqrt(tokens * SHARDS)
    count = step_count[0].astype(f32)
    offsets, total = {}, 0
    for k, cols in WIDTHS.items():
        offsets[k] = total
        total += cols

    fix = jnp.stack([1.0 - jnp.power(0.9, count), 1.0 - jnp.power(0.95, count)])
    line = Line()

    blocks, sent, flying = {}, {}, {}
    weights = (local_weight[0], adam_mean[0], adam_var[0])
    by_y = [[slice(i * rows, (i + 1) * rows)] for i in range(NY)]
    by_z = [[slice((j * NZ + i) * share, (j * NZ + i + 1) * share) for j in range(NY)] for i in range(NZ)]

    def produce(k):
        kernel = functools.partial(product_kernel, by_z if k == "e" else by_y, offsets[k])
        tiles = WIDTHS[k] // TILE
        (made, other), = line.call(
            "product", (kernel, [((half, WIDTHS[k]), bf16)] * 2, (mine_rows, sib_rows, acts)), specs=[VMEM, VMEM, ANY],
            scratch=[pltpu.VMEM((tiles, tokens, TILE), bf16), pltpu.SemaphoreType.DMA((tiles,))],
        )
        blocks[k], sent[k], flying[k] = [made, move(other, "core")], 0, None

    def terms(k):
        size = {half: rows, 3 * share: share}[blocks[k][0].shape[0]]
        at = slice(sent[k] * size, (sent[k] + 1) * size)
        came = [] if flying[k] is None else [flying[k]]
        return at, [False] * len(blocks[k]) + [True] * len(came), [*blocks[k], *came]

    def relay(k, axis):
        at, wholes, ins = terms(k)
        shape = at.stop - at.start, ins[0].shape[1]

        def done(made):
            flying[k] = move(made[0], axis)
            sent[k] += 1

        return functools.partial(relay_kernel, at, wholes), [(shape, bf16)], ins, done

    def settle(ks, axis, direct=False):
        cols = sum(WIDTHS[k] for k in ks)
        at, wholes, _ = terms(ks[0])
        ins = [a for k in ks for a in terms(k)[2]]
        if direct:
            out = [((share, cols), bf16)] * 3 + [((share, cols), f32)]
        else:
            out = [((share, cols), bf16), ((3 * share, cols), bf16)]

        def done(made):
            if direct:
                flying[ks] = [move(m, axis, -b) for m, b in zip(made, BACK[:3])]
                blocks[ks], sent[ks] = [made[3]], None
            else:
                flying[ks], blocks[ks], sent[ks] = move(made[0], axis), [made[1]], 0

        return functools.partial(settle_kernel, at, wholes, len(ks)), out, ins, done

    stepped = {}

    def adam(ks):
        start, cols = offsets[ks[0]], sum(WIDTHS[k] for k in ks)
        came = flying[ks] if sent[ks] is None else [flying[ks]]
        last = functools.partial(adam_kernel, start)

        def done(made):
            stepped[start] = made[0]

        return last, [((share, cols), f32)], (*weights, blocks[ks][0], *came), done

    def run(name, *parts, **more):
        results = line.call(name, *[p[:3] for p in parts], **more)
        for made, part in zip(results, parts):
            part[3](made)
        return results[-1]

    (mine_rows, sib_rows), = line.call(
        "pick", (functools.partial(pick_kernel, share, factor), [((half, tokens), bf16)] * 2, (out_grads,))
    )
    produce("a")
    produce("b")
    run("relay", relay("a", "y"))
    produce("e")
    run("relay", relay("b", "y"))
    run("relay", relay("e", "z"))
    produce("c")
    produce("d")
    run("relay", relay("a", "y"))
    run("relay", relay("b", "y"))
    run("relay", relay("e", "z"))
    run("relay", relay("a", "y"))
    run("relay", relay("b", "y"))
    run("relay", relay("c", "y"))
    run("relay", relay("e", "z"))
    run("relay", relay("d", "y"))
    run("settle", settle("ab", "z"))
    run("relay", relay("c", "y"))
    run("relay", relay("d", "y"))
    run("settle", settle("e", "y"))
    run("relay", relay("ab", "z"))
    run("relay", relay("e", "y"), cost=LATE_COST)
    run("relay", relay("c", "y"), cost=LATE_COST)
    run("relay", relay("d", "y"), cost=LATE_COST)
    run("relay", relay("ab", "z"), cost=LATE_COST)
    run("relay", relay("e", "y"))
    run("settle", settle("cd", "z", direct=True))
    run("adam", adam("ab"), scalars=(fix,))
    run("adam", adam("e"), scalars=(fix,))
    run("adam", adam("cd"), scalars=(fix,))
    stepped = [stepped[k] for k in sorted(stepped)]
    stepped = jnp.concatenate(stepped, axis=1)
    wide = width // workers
    parts = lax.all_to_all(stepped, "worker", split_axis=1, concat_axis=0, tiled=True)
    delta = global_weight - jnp.sum(parts.reshape(workers, share, wide), axis=0) / workers
    momentum = 0.9 * outer_momentum + delta
    updated = global_weight - 0.7 * (delta + 0.9 * momentum)
    piece = updated.astype(bf16)
    spread = jnp.broadcast_to(piece[None], (workers,) + piece.shape).reshape(workers * share, wide)
    synced = lax.all_to_all(spread, "worker", split_axis=0, concat_axis=1, tiled=True)
    return (synced, updated, momentum)


def solution(mesh):
    placed = (
        P(("worker", "shard"), None),
        P(("worker", "shard"), None),
        P("worker", "shard", None),
        P("worker", "shard", None),
        P("worker", "shard", None),
        P("shard", "worker"),
        P("shard", "worker"),
        P(),
    )
    return jax.shard_map(
        local,
        mesh=mesh,
        in_specs=placed,
        out_specs=(P("shard", None), P("shard", "worker"), P("shard", "worker")),
        check_vma=False,
    )
```

```python
import functools
import math

import jax
import jax.numpy as jnp
from jax import lax
from jax.experimental import pallas as pl
from jax.experimental.pallas import tpu as pltpu
from jax.sharding import PartitionSpec as P

WIDTHS = {"a": 2048, "b": 2048, "e": 1536, "c": 1536, "d": 1024}
TILE = 512


NZ, NY, NC = 4, 4, 2
SHARDS = NZ * NY * NC
BACK = (1, 2, 3, 0)
VMEM = pl.BlockSpec(memory_space=pltpu.VMEM)
ANY = pl.BlockSpec(memory_space=pl.ANY)
LIMIT = 12 << 20
COST = {"product": 50_000_000_000, "pick": 50_000_000_000}
OTHER_COST = 2_000_000_000
LATE_COST = 500_000_000
bf16, f32 = jnp.bfloat16, jnp.float32


def shard_of(z, y, c):
    return (z % NZ * NY + y % NY) * NC + c % NC


def sense(c):
    return 1 if c == 0 else -1


def move(array, axis, steps=1):
    pairs = []
    for z in range(NZ):
        for y in range(NY):
            for c in range(NC):
                by = steps * sense(c)
                to = {
                    "z": shard_of(z + by, y, c), "y": shard_of(z, y + by, c), "core": shard_of(z, y, c + 1)
                }[axis]
                pairs.append((shard_of(z, y, c), to))
    return lax.ppermute(array, "shard", pairs)


class Line:
    def __init__(self):
        self.last = None

    def call(self, name, *parts, scalars=(), **more):
        before = () if self.last is None else (self.last,)
        lead = len(before) + len(scalars)
        outs = [o for _, out, _ in parts for o in out]
        operands = [o for _, _, ins in parts for o in ins]

        def body(*refs):
            given, made, scratch = lead, lead + len(operands), refs[lead + len(operands) + len(outs):]
            for kernel, out, ins in parts:
                kernel(
                    *refs[len(before):lead], *refs[given:given + len(ins)], *refs[made:made + len(out)], *scratch
                )
                given, made = given + len(ins), made + len(out)

        flops = more.get("cost", COST.get(name, OTHER_COST))
        results = pl.pallas_call(
            body,
            out_shape=[jax.ShapeDtypeStruct(s, t) for s, t in outs],
            in_specs=[ANY] * len(before)
            + [pl.BlockSpec(memory_space=pltpu.SMEM)] * len(scalars)
            + (more.get("specs") or [VMEM] * len(operands)),
            out_specs=more.get("out_specs") or [VMEM] * len(outs),
            scratch_shapes=more.get("scratch", ()),
            grid=more.get("grid", ()),
            compiler_params=pltpu.CompilerParams(vmem_limit_bytes=more.get("limit", LIMIT)),
            cost_estimate=pl.CostEstimate(flops=flops, bytes_accessed=flops // 100, transcendentals=0),
            name=name,
        )(*before, *scalars, *operands)
        self.last = results[0]
        split, at = [], 0
        for _, out, _ in parts:
            split.append(results[at:at + len(out)])
            at += len(out)
        return split


def pick_kernel(share, factor, grads_ref, *outs):
    index = lax.axis_index("shard")
    y, z = (index // NC) % NY, index // (NC * NY)
    for out_ref, core in zip(outs, (index % NC, 1 - index % NC)):
        way = 1 - 2 * core
        row = lax.broadcasted_iota(jnp.int32, (out_ref.shape[0], 1), 0)
        block = row // share
        back_y, back_z = (block // NZ + 1) % NY, (block % NZ + 1) % NZ
        owner = ((z + NZ - way * back_z) % NZ * NY + (y + NY - way * back_y) % NY) * NC + core
        feature = owner * share + row % share
        place = lax.broadcasted_iota(jnp.int32, (out_ref.shape[0], grads_ref.shape[1]), 1)
        pick = jnp.where(feature == place, factor, 0.0).astype(bf16)
        out_ref[...] = lax.dot_general(
            pick, grads_ref[...], (((1,), (1,)), ((), ())), preferred_element_type=f32
        ).astype(bf16)


def product_kernel(split, first, mine_rows, sib_rows, acts_ref, mine_ref, sib_ref, held, sems):
    copies = [
        pltpu.make_async_copy(acts_ref.at[:, pl.ds(first + i * TILE, TILE)], held.at[i], sems.at[i])
        for i in range(held.shape[0])
    ]
    for copy in copies:
        copy.start()
    for i, copy in enumerate(copies):
        copy.wait()
        for start in range(0, TILE, TILE // 2):
            tile = held[i, :, start:start + TILE // 2]
            for rows_ref, out in ((sib_rows, sib_ref), (mine_rows, mine_ref)):
                total = jnp.dot(rows_ref[...], tile, preferred_element_type=f32).astype(bf16)
                at = pl.ds(i * TILE + start, TILE // 2)
                out[:, at] = jnp.concatenate([total[r] for rows in split for r in rows], axis=0)


def sum_of(at, terms):
    total = 0.0
    for ref, whole in terms:
        total += (ref[...] if whole else ref[at]).astype(f32)
    return total


def relay_kernel(at, wholes, *refs):
    refs[-1][...] = sum_of(at, zip(refs, wholes)).astype(bf16)


def settle_kernel(at, wholes, n, *refs):
    each = len(wholes)
    outs = refs[each * n:]
    start = 0
    for i in range(n):
        ins = refs[each * i:each * (i + 1)]
        part = slice(start, start + ins[0].shape[1])
        start += ins[0].shape[1]
        total = sum_of(at, zip(ins, wholes))
        row = 0
        for out in outs:
            out[:, part] = total[row:row + out.shape[0]].astype(out.dtype)
            row += out.shape[0]


def adam_kernel(start, fix_ref, weight_ref, mean_ref, var_ref, own_ref, *refs):
    came, out_ref = refs[:-1], refs[-1]
    at = pl.ds(start, own_ref.shape[1])
    grad = own_ref[own_ref.shape[0] - out_ref.shape[0]:].astype(f32)
    for ref in came:
        grad += ref[...].astype(f32)
    weight = weight_ref[:, at].astype(f32)
    moment = 0.9 * mean_ref[:, at] + 0.1 * grad
    second = 0.95 * var_ref[:, at] + 0.05 * grad * grad
    ratio = moment / fix_ref[0] / (jnp.sqrt(second / fix_ref[1]) + 1e-08)
    out_ref[...] = weight - 0.1 * (ratio + 0.1 * weight)


def local(acts, out_grads, local_weight, adam_mean, adam_var, global_weight, outer_momentum, step_count):
    workers = lax.axis_size("worker")
    tokens, width = acts.shape
    features = out_grads.shape[1]
    share = features // SHARDS
    half = features // NC
    rows = half // NY
    factor = 1.0 / math.sqrt(tokens * SHARDS)
    count = step_count[0].astype(f32)
    offsets, total = {}, 0
    for k, cols in WIDTHS.items():
        offsets[k] = total
        total += cols

    fix = jnp.stack([1.0 - jnp.power(0.9, count), 1.0 - jnp.power(0.95, count)])
    line = Line()

    blocks, sent, flying = {}, {}, {}
    weights = (local_weight[0], adam_mean[0], adam_var[0])
    by_y = [[slice(i * rows, (i + 1) * rows)] for i in range(NY)]
    by_z = [[slice((j * NZ + i) * share, (j * NZ + i + 1) * share) for j in range(NY)] for i in range(NZ)]

    def produce(k):
        kernel = functools.partial(product_kernel, by_z if k == "e" else by_y, offsets[k])
        tiles = WIDTHS[k] // TILE
        (made, other), = line.call(
            "product", (kernel, [((half, WIDTHS[k]), bf16)] * 2, (mine_rows, sib_rows, acts)), specs=[VMEM, VMEM, ANY],
            scratch=[pltpu.VMEM((tiles, tokens, TILE), bf16), pltpu.SemaphoreType.DMA((tiles,))],
        )
        blocks[k], sent[k], flying[k] = [made, move(other, "core")], 0, None

    def terms(k):
        size = {half: rows, 3 * share: share}[blocks[k][0].shape[0]]
        at = slice(sent[k] * size, (sent[k] + 1) * size)
        came = [] if flying[k] is None else [flying[k]]
        return at, [False] * len(blocks[k]) + [True] * len(came), [*blocks[k], *came]

    def relay(k, axis):
        at, wholes, ins = terms(k)
        shape = at.stop - at.start, ins[0].shape[1]

        def done(made):
            flying[k] = move(made[0], axis)
            sent[k] += 1

        return functools.partial(relay_kernel, at, wholes), [(shape, bf16)], ins, done

    def settle(ks, axis, direct=False):
        cols = sum(WIDTHS[k] for k in ks)
        at, wholes, _ = terms(ks[0])
        ins = [a for k in ks for a in terms(k)[2]]
        if direct:
            out = [((share, cols), bf16)] * 3 + [((share, cols), f32)]
        else:
            out = [((share, cols), bf16), ((3 * share, cols), bf16)]

        def done(made):
            if direct:
                flying[ks] = [move(m, axis, -b) for m, b in zip(made, BACK[:3])]
                blocks[ks], sent[ks] = [made[3]], None
            else:
                flying[ks], blocks[ks], sent[ks] = move(made[0], axis), [made[1]], 0

        return functools.partial(settle_kernel, at, wholes, len(ks)), out, ins, done

    stepped = {}

    def adam(ks):
        start, cols = offsets[ks[0]], sum(WIDTHS[k] for k in ks)
        came = flying[ks] if sent[ks] is None else [flying[ks]]
        last = functools.partial(adam_kernel, start)

        def done(made):
            stepped[start] = made[0]

        return last, [((share, cols), f32)], (*weights, blocks[ks][0], *came), done

    def run(name, *parts, **more):
        results = line.call(name, *[p[:3] for p in parts], **more)
        for made, part in zip(results, parts):
            part[3](made)
        return results[-1]

    (mine_rows, sib_rows), = line.call(
        "pick", (functools.partial(pick_kernel, share, factor), [((half, tokens), bf16)] * 2, (out_grads,))
    )
    produce("a")
    produce("b")
    run("relay", relay("a", "y"))
    produce("e")
    run("relay", relay("b", "y"))
    run("relay", relay("e", "z"))
    produce("c")
    produce("d")
    run("relay", relay("a", "y"))
    run("relay", relay("b", "y"))
    run("relay", relay("e", "z"))
    run("relay", relay("a", "y"))
    run("relay", relay("b", "y"))
    run("relay", relay("c", "y"))
    run("relay", relay("e", "z"))
    run("relay", relay("d", "y"))
    run("settle", settle("ab", "z"))
    run("relay", relay("c", "y"))
    run("relay", relay("d", "y"))
    run("settle", settle("e", "y"))
    run("relay", relay("ab", "z"))
    run("relay", relay("c", "y"), cost=LATE_COST)
    run("relay", relay("e", "y"), cost=LATE_COST)
    run("relay", relay("d", "y"))
    run("relay", relay("ab", "z"), cost=LATE_COST)
    run("relay", relay("e", "y"))
    run("settle", settle("cd", "z", direct=True))
    run("adam", adam("ab"), scalars=(fix,))
    run("adam", adam("e"), scalars=(fix,))
    run("adam", adam("cd"), scalars=(fix,))
    stepped = [stepped[k] for k in sorted(stepped)]
    stepped = jnp.concatenate(stepped, axis=1)
    wide = width // workers
    parts = lax.all_to_all(stepped, "worker", split_axis=1, concat_axis=0, tiled=True)
    delta = global_weight - jnp.sum(parts.reshape(workers, share, wide), axis=0) / workers
    momentum = 0.9 * outer_momentum + delta
    updated = global_weight - 0.7 * (delta + 0.9 * momentum)
    piece = updated.astype(bf16)
    spread = jnp.broadcast_to(piece[None], (workers,) + piece.shape).reshape(workers * share, wide)
    synced = lax.all_to_all(spread, "worker", split_axis=0, concat_axis=1, tiled=True)
    return (synced, updated, momentum)


def solution(mesh):
    placed = (
        P(("worker", "shard"), None),
        P(("worker", "shard"), None),
        P("worker", "shard", None),
        P("worker", "shard", None),
        P("worker", "shard", None),
        P("shard", "worker"),
        P("shard", "worker"),
        P(),
    )
    return jax.shard_map(
        local,
        mesh=mesh,
        in_specs=placed,
        out_specs=(P("shard", None), P("shard", "worker"), P("shard", "worker")),
        check_vma=False,
    )
```

```python
import functools
import math

import jax
import jax.numpy as jnp
from jax import lax
from jax.experimental import pallas as pl
from jax.experimental.pallas import tpu as pltpu
from jax.sharding import PartitionSpec as P

WIDTHS = {"a": 2048, "b": 2048, "e": 1536, "c": 1536, "d": 1024}
TILE = 512


NZ, NY, NC = 4, 4, 2
SHARDS = NZ * NY * NC
BACK = (1, 2, 3, 0)
VMEM = pl.BlockSpec(memory_space=pltpu.VMEM)
ANY = pl.BlockSpec(memory_space=pl.ANY)
LIMIT = 12 << 20
COST = {"product": 50_000_000_000, "pick": 50_000_000_000}
OTHER_COST = 2_000_000_000
LATE_COST = 500_000_000
bf16, f32 = jnp.bfloat16, jnp.float32


def shard_of(z, y, c):
    return (z % NZ * NY + y % NY) * NC + c % NC


def sense(c):
    return 1 if c == 0 else -1


def move(array, axis, steps=1):
    pairs = []
    for z in range(NZ):
        for y in range(NY):
            for c in range(NC):
                by = steps * sense(c)
                to = {
                    "z": shard_of(z + by, y, c), "y": shard_of(z, y + by, c), "core": shard_of(z, y, c + 1)
                }[axis]
                pairs.append((shard_of(z, y, c), to))
    return lax.ppermute(array, "shard", pairs)


class Line:
    def __init__(self):
        self.last = None

    def call(self, name, *parts, scalars=(), **more):
        before = () if self.last is None else (self.last,)
        lead = len(before) + len(scalars)
        outs = [o for _, out, _ in parts for o in out]
        operands = [o for _, _, ins in parts for o in ins]

        def body(*refs):
            given, made, scratch = lead, lead + len(operands), refs[lead + len(operands) + len(outs):]
            for kernel, out, ins in parts:
                kernel(
                    *refs[len(before):lead], *refs[given:given + len(ins)], *refs[made:made + len(out)], *scratch
                )
                given, made = given + len(ins), made + len(out)

        flops = more.get("cost", COST.get(name, OTHER_COST))
        results = pl.pallas_call(
            body,
            out_shape=[jax.ShapeDtypeStruct(s, t) for s, t in outs],
            in_specs=[ANY] * len(before)
            + [pl.BlockSpec(memory_space=pltpu.SMEM)] * len(scalars)
            + (more.get("specs") or [VMEM] * len(operands)),
            out_specs=more.get("out_specs") or [VMEM] * len(outs),
            scratch_shapes=more.get("scratch", ()),
            grid=more.get("grid", ()),
            compiler_params=pltpu.CompilerParams(vmem_limit_bytes=more.get("limit", LIMIT)),
            cost_estimate=pl.CostEstimate(flops=flops, bytes_accessed=flops // 100, transcendentals=0),
            name=name,
        )(*before, *scalars, *operands)
        self.last = results[0]
        split, at = [], 0
        for _, out, _ in parts:
            split.append(results[at:at + len(out)])
            at += len(out)
        return split


def pick_kernel(share, factor, grads_ref, *outs):
    index = lax.axis_index("shard")
    y, z = (index // NC) % NY, index // (NC * NY)
    for out_ref, core in zip(outs, (index % NC, 1 - index % NC)):
        way = 1 - 2 * core
        row = lax.broadcasted_iota(jnp.int32, (out_ref.shape[0], 1), 0)
        block = row // share
        back_y, back_z = (block // NZ + 1) % NY, (block % NZ + 1) % NZ
        owner = ((z + NZ - way * back_z) % NZ * NY + (y + NY - way * back_y) % NY) * NC + core
        feature = owner * share + row % share
        place = lax.broadcasted_iota(jnp.int32, (out_ref.shape[0], grads_ref.shape[1]), 1)
        pick = jnp.where(feature == place, factor, 0.0).astype(bf16)
        out_ref[...] = lax.dot_general(
            pick, grads_ref[...], (((1,), (1,)), ((), ())), preferred_element_type=f32
        ).astype(bf16)


def product_kernel(split, first, mine_rows, sib_rows, acts_ref, mine_ref, sib_ref, held, sems):
    copies = [
        pltpu.make_async_copy(acts_ref.at[:, pl.ds(first + i * TILE, TILE)], held.at[i], sems.at[i])
        for i in range(held.shape[0])
    ]
    for copy in copies:
        copy.start()
    for i, copy in enumerate(copies):
        copy.wait()
        for start in range(0, TILE, TILE // 2):
            tile = held[i, :, start:start + TILE // 2]
            for rows_ref, out in ((sib_rows, sib_ref), (mine_rows, mine_ref)):
                total = jnp.dot(rows_ref[...], tile, preferred_element_type=f32).astype(bf16)
                at = pl.ds(i * TILE + start, TILE // 2)
                out[:, at] = jnp.concatenate([total[r] for rows in split for r in rows], axis=0)


def sum_of(at, terms):
    total = 0.0
    for ref, whole in terms:
        total += (ref[...] if whole else ref[at]).astype(f32)
    return total


def relay_kernel(at, wholes, *refs):
    refs[-1][...] = sum_of(at, zip(refs, wholes)).astype(bf16)


def settle_kernel(at, wholes, n, *refs):
    each = len(wholes)
    outs = refs[each * n:]
    start = 0
    for i in range(n):
        ins = refs[each * i:each * (i + 1)]
        part = slice(start, start + ins[0].shape[1])
        start += ins[0].shape[1]
        total = sum_of(at, zip(ins, wholes))
        row = 0
        for out in outs:
            out[:, part] = total[row:row + out.shape[0]].astype(out.dtype)
            row += out.shape[0]


def adam_kernel(start, fix_ref, weight_ref, mean_ref, var_ref, own_ref, *refs):
    came, out_ref = refs[:-1], refs[-1]
    at = pl.ds(start, own_ref.shape[1])
    grad = own_ref[own_ref.shape[0] - out_ref.shape[0]:].astype(f32)
    for ref in came:
        grad += ref[...].astype(f32)
    weight = weight_ref[:, at].astype(f32)
    moment = 0.9 * mean_ref[:, at] + 0.1 * grad
    second = 0.95 * var_ref[:, at] + 0.05 * grad * grad
    ratio = moment / fix_ref[0] / (jnp.sqrt(second / fix_ref[1]) + 1e-08)
    out_ref[...] = weight - 0.1 * (ratio + 0.1 * weight)


def local(acts, out_grads, local_weight, adam_mean, adam_var, global_weight, outer_momentum, step_count):
    workers = lax.axis_size("worker")
    tokens, width = acts.shape
    features = out_grads.shape[1]
    share = features // SHARDS
    half = features // NC
    rows = half // NY
    factor = 1.0 / math.sqrt(tokens * SHARDS)
    count = step_count[0].astype(f32)
    offsets, total = {}, 0
    for k, cols in WIDTHS.items():
        offsets[k] = total
        total += cols

    fix = jnp.stack([1.0 - jnp.power(0.9, count), 1.0 - jnp.power(0.95, count)])
    line = Line()

    blocks, sent, flying = {}, {}, {}
    weights = (local_weight[0], adam_mean[0], adam_var[0])
    by_y = [[slice(i * rows, (i + 1) * rows)] for i in range(NY)]
    by_z = [[slice((j * NZ + i) * share, (j * NZ + i + 1) * share) for j in range(NY)] for i in range(NZ)]

    def produce(k):
        kernel = functools.partial(product_kernel, by_z if k == "e" else by_y, offsets[k])
        tiles = WIDTHS[k] // TILE
        (made, other), = line.call(
            "product", (kernel, [((half, WIDTHS[k]), bf16)] * 2, (mine_rows, sib_rows, acts)), specs=[VMEM, VMEM, ANY],
            scratch=[pltpu.VMEM((tiles, tokens, TILE), bf16), pltpu.SemaphoreType.DMA((tiles,))],
        )
        blocks[k], sent[k], flying[k] = [made, move(other, "core")], 0, None

    def terms(k):
        size = {half: rows, 3 * share: share}[blocks[k][0].shape[0]]
        at = slice(sent[k] * size, (sent[k] + 1) * size)
        came = [] if flying[k] is None else [flying[k]]
        return at, [False] * len(blocks[k]) + [True] * len(came), [*blocks[k], *came]

    def relay(k, axis):
        at, wholes, ins = terms(k)
        shape = at.stop - at.start, ins[0].shape[1]

        def done(made):
            flying[k] = move(made[0], axis)
            sent[k] += 1

        return functools.partial(relay_kernel, at, wholes), [(shape, bf16)], ins, done

    def settle(ks, axis, direct=False):
        cols = sum(WIDTHS[k] for k in ks)
        at, wholes, _ = terms(ks[0])
        ins = [a for k in ks for a in terms(k)[2]]
        if direct:
            out = [((share, cols), bf16)] * 3 + [((share, cols), f32)]
        else:
            out = [((share, cols), bf16), ((3 * share, cols), bf16)]

        def done(made):
            if direct:
                flying[ks] = [move(m, axis, -b) for m, b in zip(made, BACK[:3])]
                blocks[ks], sent[ks] = [made[3]], None
            else:
                flying[ks], blocks[ks], sent[ks] = move(made[0], axis), [made[1]], 0

        return functools.partial(settle_kernel, at, wholes, len(ks)), out, ins, done

    stepped = {}

    def adam(ks):
        start, cols = offsets[ks[0]], sum(WIDTHS[k] for k in ks)
        came = flying[ks] if sent[ks] is None else [flying[ks]]
        last = functools.partial(adam_kernel, start)

        def done(made):
            stepped[start] = made[0]

        return last, [((share, cols), f32)], (*weights, blocks[ks][0], *came), done

    def run(name, *parts, **more):
        results = line.call(name, *[p[:3] for p in parts], **more)
        for made, part in zip(results, parts):
            part[3](made)
        return results[-1]

    (mine_rows, sib_rows), = line.call(
        "pick", (functools.partial(pick_kernel, share, factor), [((half, tokens), bf16)] * 2, (out_grads,))
    )
    produce("a")
    produce("b")
    run("relay", relay("a", "y"))
    produce("e")
    run("relay", relay("b", "y"))
    run("relay", relay("e", "z"))
    produce("c")
    produce("d")
    run("relay", relay("a", "y"))
    run("relay", relay("b", "y"))
    run("relay", relay("e", "z"))
    run("relay", relay("a", "y"))
    run("relay", relay("b", "y"))
    run("relay", relay("c", "y"))
    run("relay", relay("e", "z"))
    run("relay", relay("d", "y"))
    run("settle", settle("ab", "z"))
    run("relay", relay("c", "y"))
    run("relay", relay("d", "y"))
    run("settle", settle("e", "y"))
    run("relay", relay("ab", "z"))
    run("relay", relay("c", "y"), cost=LATE_COST)
    run("relay", relay("d", "y"), cost=LATE_COST)
    run("relay", relay("e", "y"))
    run("relay", relay("ab", "z"), cost=LATE_COST)
    run("relay", relay("e", "y"))
    run("settle", settle("cd", "z", direct=True))
    run("adam", adam("ab"), scalars=(fix,))
    run("adam", adam("e"), scalars=(fix,))
    run("adam", adam("cd"), scalars=(fix,))
    stepped = [stepped[k] for k in sorted(stepped)]
    stepped = jnp.concatenate(stepped, axis=1)
    wide = width // workers
    parts = lax.all_to_all(stepped, "worker", split_axis=1, concat_axis=0, tiled=True)
    delta = global_weight - jnp.sum(parts.reshape(workers, share, wide), axis=0) / workers
    momentum = 0.9 * outer_momentum + delta
    updated = global_weight - 0.7 * (delta + 0.9 * momentum)
    piece = updated.astype(bf16)
    spread = jnp.broadcast_to(piece[None], (workers,) + piece.shape).reshape(workers * share, wide)
    synced = lax.all_to_all(spread, "worker", split_axis=0, concat_axis=1, tiled=True)
    return (synced, updated, momentum)


def solution(mesh):
    placed = (
        P(("worker", "shard"), None),
        P(("worker", "shard"), None),
        P("worker", "shard", None),
        P("worker", "shard", None),
        P("worker", "shard", None),
        P("shard", "worker"),
        P("shard", "worker"),
        P(),
    )
    return jax.shard_map(
        local,
        mesh=mesh,
        in_specs=placed,
        out_specs=(P("shard", None), P("shard", "worker"), P("shard", "worker")),
        check_vma=False,
    )
```
